768 devices in a mesh: dp: 96 (over x, z, core), expert: 8 (over y).
Axes of the slice: x: 4, y: 8, z: 12, core: 2. Of those that a mesh axis runs over, the one named last changes fastest.
Arguments:
- grad_out: bfloat16 [30720, 3840], P(('dp', 'expert')), may hold values from -2.5 to 2.5
- routing: int32 [30720, 8], P(('dp', 'expert')), may hold values from 0 to 15, as said below
- probs: bfloat16 [30720, 8], P(('dp', 'expert')), may hold values from 0.099609375 to 1
- down_weight: bfloat16 [3840, 2048], P('dp', 'expert'), may hold values from -0.1875 to 0.1875
- gate_saved: bfloat16 [768, 30, 2048], P('dp', None, 'expert'), may hold values from -6 to 6
- up_saved: bfloat16 [768, 30, 2048], P('dp', None, 'expert'), may hold values from -6 to 6
Outputs:
- down_grad: float32 [3840, 2048], P('dp', 'expert')
- gate_grad: bfloat16 [768, 30, 2048], P('dp', None, 'expert')
- up_grad: bfloat16 [768, 30, 2048], P('dp', None, 'expert')
- prob_grad: float32 [30720, 8], P(('dp', 'expert'))
The draws below stay inside these ranges and needn't reach their ends.
Inputs may be any that keep to these rules, and one draw needn't show every extreme that they name: `routing`: each row names 8 different experts; among one device's 40 tokens at most 30 name any one expert below 2; in every draw on some index of dp all devices' tokens name one such expert exactly 30 times.
All inputs are finite; a program needn't handle non-finite values.
Results may differ from the reference program's by a relative error of at most 0.003.
Values may be sent and summed in bfloat16 or wider, within the bound.
A program may use at most 32 MiB of HBM per device.

```python
import jax
import jax.numpy as jnp
from jax import lax

D_WIN = 3840
FF_WIN = 1024
BUCKET = 16
TOP = 8
FLIGHT = 2
TOK_DEV = 40
CAP = 30
TOKENS = 30720
N_DP = 96
N_EXPERT = 8


def draw_routing(key, part):
    key = jax.random.fold_in(key, 11)
    blocks = TOKENS // TOK_DEV
    keys = jax.random.split(key, 6)
    lowest = max(1, CAP // 3)
    counts = jax.random.randint(keys[0], (blocks, FLIGHT), lowest, CAP + 1)
    full_row = jax.random.randint(keys[1], (), 0, N_DP)
    full_exp = jax.random.randint(keys[2], (), 0, FLIGHT)
    block_row = jnp.arange(blocks, dtype=jnp.int32) // N_EXPERT
    force = (block_row == full_row)[:, None] & (jnp.arange(FLIGHT, dtype=jnp.int32)[None, :] == full_exp)
    counts = jnp.where(force, CAP, counts)
    scores = jax.random.randint(keys[3], (blocks, FLIGHT, TOK_DEV), 0, 1 << 20) * TOK_DEV + jnp.arange(TOK_DEV, dtype=jnp.int32)
    ranks = jnp.argsort(jnp.argsort(scores, axis=-1), axis=-1)
    chosen = ranks < counts[:, :, None]
    chosen_tok = jnp.transpose(chosen, (0, 2, 1)).reshape(TOKENS, FLIGHT)
    n_in = jnp.sum(chosen_tok.astype(jnp.int32), axis=1)
    others = BUCKET - FLIGHT
    other_score = jax.random.randint(keys[4], (TOKENS, others), 0, 1 << 20) * BUCKET + jnp.arange(others, dtype=jnp.int32)
    other_perm = jnp.argsort(other_score, axis=-1).astype(jnp.int32) + FLIGHT
    valid_other = jnp.arange(others, dtype=jnp.int32)[None, :] < (TOP - n_in)[:, None]
    candidates = jnp.concatenate([jnp.broadcast_to(jnp.arange(FLIGHT, dtype=jnp.int32), (TOKENS, FLIGHT)), other_perm], axis=1)
    valid = jnp.concatenate([chosen_tok, valid_other], axis=1)
    pick_score = jax.random.randint(keys[5], (TOKENS, BUCKET), 0, 1 << 20) * BUCKET + jnp.arange(BUCKET, dtype=jnp.int32)
    sort_key = jnp.where(valid, pick_score, pick_score + (1 << 26))
    order = jnp.argsort(sort_key, axis=-1)[:, :TOP]
    return jnp.take_along_axis(candidates, order, axis=1).astype(jnp.int32)


def strengthened(array, rng, source, target, shards_of, factor):
    def block_of(dim):
        return (jnp.arange(array.shape[dim]) // (array.shape[dim] // shards_of)).reshape((-1,) + (1,) * (array.ndim - 1 - dim))

    one_side = jax.random.permutation(rng, shards_of)[block_of(target)]
    far = (block_of(target) + shards_of // 2) % shards_of
    return jnp.where((block_of(source) == one_side) | (block_of(source) == far), factor * array, array)


def level_of(key, dims, cuts, low, high):
    factor_of, own = 1.0, jax.random.fold_in(key, 6)
    for dim, shards_of in cuts:
        draws = jnp.exp(jax.random.uniform(jax.random.fold_in(own, dim), (shards_of,), jnp.float32, low / len(cuts), high / len(cuts)))
        factor_of = factor_of * jnp.repeat(draws, dims[dim] // shards_of).reshape([-1 if axis == dim else 1 for axis in range(len(dims))])
    return factor_of


def bell_draw(own_key, dims, scale, reach, cuts=(), kind=jnp.bfloat16):
    result = jax.random.normal(own_key, dims, jnp.float32) * scale
    if len(cuts) > 0:
        result = level_of(own_key, dims, cuts, -0.22, 0.18) * result
    return jnp.clip(result, min=-reach, max=reach).astype(kind)


def gaussian_with(key, shape, deviation, limit, cuts, heavy, kind=jnp.bfloat16):
    array = deviation * jax.random.normal(key, shape, jnp.float32)
    if cuts:
        array = array * level_of(key, shape, cuts, -0.22, 0.18)
    return jnp.clip(strengthened(array, jax.random.fold_in(key, 3), *heavy), -limit, limit).astype(kind)


def setup_inputs(seed: int = 0) -> dict:
    key_of = jax.random.split(jax.random.key(seed), 7)
    grad_out = gaussian_with(key_of[0], (TOKENS, D_WIN), 0.1, 2.5, ((0, 768),), (0, 1, 768, 6.0))
    routing = draw_routing(jax.random.fold_in(key_of[6], 71), 0)
    probs = jnp.clip(0.099609375 + 0.9003906 * jax.random.uniform(key_of[2], (TOKENS, TOP), jnp.float32) ** level_of(key_of[2], (TOKENS, TOP), ((0, 768),), -0.2, 0.2), 0.099609375, 1.0).astype(jnp.bfloat16)
    down_weight = bell_draw(key_of[3], (D_WIN, FLIGHT * FF_WIN), FF_WIN ** -0.5, 0.1875, ((0, 96), (1, 8)))
    gate_saved = bell_draw(key_of[4], (N_DP * N_EXPERT, CAP, FLIGHT * FF_WIN), 1.0, 6.0, ((0, 96), (2, 8)))
    up_saved = bell_draw(key_of[5], (N_DP * N_EXPERT, CAP, FLIGHT * FF_WIN), 1.0, 6.0, ((0, 96), (2, 8)))
    return dict(grad_out=grad_out, routing=routing, probs=probs, down_weight=down_weight, gate_saved=gate_saved, up_saved=up_saved)


def slot_tables(route, expert):
    hit = route == expert
    onrow = jnp.any(hit, axis=-1)
    slot = jnp.cumsum(onrow.astype(jnp.int32), axis=-1) - 1
    table = (slot[..., None, :] == jnp.arange(CAP, dtype=jnp.int32)[:, None]) & onrow[..., None, :]
    return hit, table.astype(jnp.float32)


def reference(grad_out, routing, probs, down_weight, gate_saved, up_saved):
    blocks = TOKENS // TOK_DEV
    route = routing.reshape(blocks, TOK_DEV, TOP)
    prob = probs.astype(jnp.float32).reshape(blocks, TOK_DEV, TOP)
    rows_in = grad_out.astype(jnp.float32).reshape(blocks, TOK_DEV, D_WIN)
    grads = []
    gates = []
    ups = []
    prob_grad = jnp.zeros((blocks, TOK_DEV, TOP), jnp.float32)
    for expert in range(FLIGHT):
        hit, table = slot_tables(route, expert)
        weight = jnp.sum(jnp.where(hit, prob, jnp.float32(0.0)), axis=-1)
        rows = jnp.einsum("bct,btd->bcd", table, rows_in).astype(jnp.bfloat16).reshape(-1, D_WIN)
        slot_prob = jnp.einsum("bct,bt->bc", table, weight, precision=lax.Precision.HIGHEST).reshape(-1, 1)
        lower = expert * FF_WIN
        dh = jnp.dot(rows, down_weight[:, lower:lower + FF_WIN], preferred_element_type=jnp.float32)
        gate = gate_saved[:, :, lower:lower + FF_WIN].reshape(-1, FF_WIN).astype(jnp.float32)
        upper = up_saved[:, :, lower:lower + FF_WIN].reshape(-1, FF_WIN).astype(jnp.float32)
        sig = jax.nn.sigmoid(gate)
        act = gate * sig
        hidden = act * upper
        scaled = slot_prob * dh
        ups.append((scaled * act).astype(jnp.bfloat16).reshape(blocks, CAP, FF_WIN))
        gates.append((scaled * upper * sig * (1.0 + gate * (1.0 - sig))).astype(jnp.bfloat16).reshape(blocks, CAP, FF_WIN))
        weighted = (slot_prob * hidden).astype(jnp.bfloat16)
        grads.append(lax.dot_general(rows, weighted, (((0,), (0,)), ((), ())), preferred_element_type=jnp.float32))
        value = jnp.sum(hidden * dh, axis=-1).reshape(blocks, CAP)
        tok_val = jnp.einsum("bct,bc->bt", table, value, precision=lax.Precision.HIGHEST)
        prob_grad = prob_grad + jnp.where(hit, tok_val[..., None], jnp.float32(0.0))
    return (jnp.concatenate(grads, axis=1), jnp.concatenate(gates, axis=2),
            jnp.concatenate(ups, axis=2), prob_grad.reshape(TOKENS, TOP))
```

```python
import functools

import jax
import jax.numpy as jnp
from jax import lax
from jax.experimental import pallas as pl
from jax.experimental.pallas import tpu as pltpu
from jax.sharding import PartitionSpec as P

FLIGHT = 2
NX = 4
H = 2
F32 = jnp.float32
BF16 = jnp.bfloat16


def kernel(
    cfg,
    tok_ref, route_ref, prob_ref, w_ref, gate_ref, up_ref,
    dg_ref, gg_ref, ug_ref, pg_ref,
    yb, meta, wt, gt, ut, pt, wo, wg, pb, cr, xs, xr, zs, zr, ac, vs, vr,
    y_send, y_recv, m_send, m_recv, wc_send, wc_recv, wz_send, wz_recv, wx_send, wx_recv,
    c_send, c_recv, x_send, x_recv, z_send, z_recv, v_send, v_recv,
):
    ny, nz = cfg
    toks, width = tok_ref.shape
    slots, hid = gate_ref.shape[1], gate_ref.shape[2]
    half = hid // 2
    nzh = nz // H
    chan = nzh * 2 * toks
    lanes = yb.shape[-1]
    n_chunks = NX * H

    d = lax.axis_index("dp")
    y = lax.axis_index("expert")
    x = lax.div(d, 2 * nz)
    z = lax.rem(lax.div(d, 2), nz)
    c = lax.rem(d, 2)
    expert0 = lax.div(y, ny // FLIGHT) == 0

    def at_x(i):
        return (lax.rem(x + i, NX) * nz + z) * 2 + c, y

    def at_z(zz):
        return (x * nz + zz) * 2 + c, y

    def at_y(i):
        return d, lax.rem(y + i, ny)

    other_core = ((x * nz + z) * 2 + (1 - c), y)

    def remote(src, dst, send, recv, to):
        return pltpu.make_async_remote_copy(
            src_ref=src, dst_ref=dst, send_sem=send, recv_sem=recv,
            device_id=to, device_id_type=pl.DeviceIdType.MESH,
        )

    barrier = pltpu.get_barrier_semaphore()
    partners = [other_core]
    partners += [at_x(i) for i in range(1, NX)]
    partners += [at_z(lax.rem(z + i, nz)) for i in range(1, nz)]
    partners += [at_y(i) for i in range(1, ny)]
    for to in partners:
        pl.semaphore_signal(barrier, inc=1, device_id=to, device_id_type=pl.DeviceIdType.MESH)

    sub = lax.broadcasted_iota(jnp.int32, (toks, 128), 0)
    lane = lax.broadcasted_iota(jnp.int32, (toks, 128), 1)
    eye = sub == lane

    def to_row(col):
        return jnp.sum(jnp.where(eye, col, 0.0), axis=0, keepdims=True)

    def to_col(row):
        return jnp.sum(jnp.where(eye, row, 0.0), axis=1, keepdims=True)

    route = route_ref[...]
    prob = prob_ref[...].astype(F32)
    rows = []
    for e in range(FLIGHT):
        hit = route == e
        on = jnp.sum(jnp.where(hit, 1.0, 0.0), axis=1, keepdims=True)
        weight = jnp.sum(jnp.where(hit, prob, 0.0), axis=1, keepdims=True)
        before = jnp.sum(jnp.where(lane < sub, to_row(on), 0.0), axis=1, keepdims=True)
        rows += [to_row(weight), to_row(jnp.where(on > 0.0, before, -1.0))]
    line = lax.broadcasted_iota(jnp.int32, (8, 128), 0)
    tile = jnp.zeros((8, 128), F32)
    for i, row in enumerate(rows):
        tile = jnp.where(line == i, row, tile)
    meta[y] = tile

    for k in range(NX):
        for h in range(H):
            pieces = []
            for i in range(nzh):
                start = ((k * nz) + i * H + h) * 2 * toks
                pieces.append(tok_ref[:, start:start + 2 * toks].astype(F32))
            if lanes > chan:
                pieces.append(jnp.zeros((toks, lanes - chan), F32))
            yb[k, h, y] = jnp.concatenate(pieces, axis=1).astype(BF16)

    pl.semaphore_wait(barrier, len(partners))

    def target_x(q):
        return lax.rem(x + 1 + q % NX, NX)

    def hops(q, way):
        return ny // 2 if (q + way) % 2 == 0 else ny // 2 - 1

    def ring(q, way, s):
        block = lax.rem(y + ny - s, ny) if way == 0 else lax.rem(y + s, ny)
        ref = yb.at[target_x(q), q // NX, block]
        return remote(
            ref, ref, y_send.at[q, way, s], y_recv.at[q, way, s], at_y(1 if way == 0 else ny - 1)
        )

    meta_copies = [
        remote(meta.at[y], meta.at[y], m_send.at[i - 1], m_recv.at[i - 1], at_y(i))
        for i in range(1, ny)
    ]
    w_pair = remote(w_ref, wo, wc_send.at[0], wc_recv.at[0], other_core)
    zh, zi = lax.rem(z, H), lax.div(z, H)
    w_own = wg.at[c, x, zh, zi]
    w_z = [
        remote(w_own, w_own, wz_send.at[i - 1], wz_recv.at[i - 1], at_z(lax.rem(z + i, nz)))
        for i in range(1, nz)
    ]
    w_x = [
        remote(wg.at[c, x], wg.at[c, x], wx_send.at[i], wx_recv.at[i], at_x(1 if i == 0 else NX - 1))
        for i in range(2)
    ]
    w_relay = []
    for i in range(2):
        ref = wg.at[c, lax.rem(x + (NX - 1 if i == 0 else 1), NX), i]
        w_relay.append(
            remote(ref, ref, wx_send.at[2 + i], wx_recv.at[2 + i], at_x(1 if i == 0 else NX - 1))
        )
    w_core = remote(wg.at[c], wg.at[c], wc_send.at[1], wc_recv.at[1], other_core)
    core_copies = [
        remote(pb.at[q, 1 - c], cr.at[q], c_send.at[q], c_recv.at[q], other_core)
        for q in range(n_chunks)
    ]
    x_copies = {
        q: remote(
            xs.at[q // NX, q % NX], xr.at[q // NX, q % NX],
            x_send.at[q // NX, q % NX], x_recv.at[q // NX, q % NX], at_x(1 + q % NX),
        )
        for q in range(n_chunks) if q % NX < NX - 1
    }
    value_copies = [
        remote(
            vs.at[lax.rem(y + i, ny)], vr.at[y], v_send.at[i - 1], v_recv.at[i - 1], at_y(i)
        )
        for i in range(1, ny)
    ]

    def z_copy(h, i):
        return remote(
            zs.at[h, i], zr.at[z], z_send.at[h, i], z_recv.at[z], at_z(i * H + h)
        )

    def row_of(source, field):
        both = meta[source]
        return jnp.where(expert0, both[field:field + 1], both[2 + field:3 + field])

    def spread():
        for copy in meta_copies:
            copy.wait_recv()
        for s in range(ny):
            slot_col = to_col(row_of(s, 1))
            p_col = to_col(row_of(s, 0))
            slot_lane = lax.broadcasted_iota(jnp.int32, (toks, slots), 1).astype(F32)
            table = jnp.where(slot_col == slot_lane, 1.0, 0.0).astype(BF16)
            g = jnp.dot(table, gate_ref[s], preferred_element_type=F32)
            u = jnp.dot(table, up_ref[s], preferred_element_type=F32)
            gt[s] = g
            ut[s] = u
            pt[s] = jnp.broadcast_to(p_col, (toks, 128))
            hidden = g * jax.nn.sigmoid(g) * u
            wt[pl.ds(s * toks, toks), :] = p_col * hidden

    def tokens_of(k, h):
        return yb[k, h].astype(F32).reshape(ny * toks, lanes).astype(BF16)

    def multiply(q):
        for way in range(2):
            if hops(q, way):
                ring(q, way, hops(q, way) - 1).wait_recv()
        part = lax.dot_general(
            tokens_of(target_x(q), q // NX), wt[...].astype(BF16), (((0,), (0,)), ((), ())),
            preferred_element_type=F32,
        )
        for i in range(nzh):
            for j in range(2):
                lo = (i * 2 + j) * toks
                pb[q, j, i] = part[lo:lo + toks]
        core_copies[q].start()

    def pair(q):
        h, j = q // NX, q % NX
        core_copies[q].wait_recv()
        total = pb[q, c] + cr[q]
        if j < NX - 1:
            xs[h, j] = total.astype(BF16)
            x_copies[q].start()
            return
        for i in range(NX - 1):
            x_copies[h * NX + i].wait_recv()
            total = total + xr[h, i].astype(F32)
        ac[h] = total
        zs[h] = total.astype(BF16)
        for i in range(nzh):
            @pl.when(z != i * H + h)
            def _():
                z_copy(h, i).start()

    def w_first():
        w_pair.wait_recv()
        mine = w_ref[...].astype(F32)
        theirs = wo[...].astype(F32)
        first = jnp.where(c == 0, mine, theirs)
        second = jnp.where(c == 0, theirs, mine)
        both = jnp.concatenate([first, second], axis=0)
        wg[c, x, zh, zi] = jnp.where(c == 0, both[:, :half], both[:, half:]).astype(BF16)
        for copy in w_z:
            copy.start()

    def w_second():
        for copy in w_z:
            copy.wait_recv()
        for copy in w_x:
            copy.start()

    def w_third():
        for copy, relay in zip(w_x, w_relay):
            copy.wait_recv()
            relay.start()

    def w_fourth():
        for relay in w_relay:
            relay.wait_recv()
        w_core.start()

    def activations():
        w_core.wait_recv()
        dh = jnp.zeros((ny * toks, hid), F32)
        for k in range(NX):
            for h in range(H):
                weights = jnp.concatenate(
                    [wg[i, k, h].reshape(chan, half) for i in range(2)], axis=1
                )
                dh = dh + jnp.dot(
                    tokens_of(k, h)[:, :chan], weights, preferred_element_type=F32
                )
        for s in range(ny):
            dh_s = dh[s * toks:(s + 1) * toks]
            g, u, p = gt[s], ut[s], pt[s][:, :1]
            sig = jax.nn.sigmoid(g)
            act = g * sig
            hidden = act * u
            scaled = p * dh_s
            up_tok = (scaled * act).astype(BF16)
            gate_tok = (scaled * u * sig * (1.0 + g * (1.0 - sig))).astype(BF16)
            slot_line = lax.broadcasted_iota(jnp.int32, (slots, toks), 0).astype(F32)
            pack = jnp.where(row_of(s, 1)[:, :toks] == slot_line, 1.0, 0.0).astype(BF16)
            ug_ref[s] = jnp.dot(pack, up_tok, preferred_element_type=F32).astype(BF16)
            gg_ref[s] = jnp.dot(pack, gate_tok, preferred_element_type=F32).astype(BF16)
            value = to_row(jnp.sum(hidden * dh_s, axis=1, keepdims=True))
            vs[s] = jnp.broadcast_to(value, (8, 128))
        for copy in value_copies:
            copy.start()
        vr[y] = vs[y]

    w_pair.start()
    for copy in meta_copies:
        copy.start()
    depth = ny // 2
    for way in range(2):
        if hops(0, way):
            ring(0, way, 0).start()
    for t in range(n_chunks + depth + 1):
        if t + 1 < n_chunks:
            for way in range(2):
                if hops(t + 1, way):
                    ring(t + 1, way, 0).start()
        if t == 0:
            w_first()
        for s in range(depth - 1, 0, -1):
            q = t - s
            if 0 <= q < n_chunks:
                for way in range(2):
                    if s < hops(q, way):
                        ring(q, way, s - 1).wait_recv()
                        ring(q, way, s).start()
        if t == 0:
            spread()
        if t == 3:
            w_second()
        if t == 6:
            w_third()
        if t == 8:
            w_fourth()
        q = t - depth
        if 0 <= q < n_chunks:
            multiply(q)
        q = t - depth - 1
        if 0 <= q < n_chunks:
            pair(q)
    activations()

    for copy in value_copies:
        copy.wait_recv()
    held = jnp.zeros((toks, route.shape[1]), F32)
    share = ny // FLIGHT
    for e in range(FLIGHT):
        row = vr[e * share][0:1]
        for i in range(1, share):
            row = row + vr[e * share + i][0:1]
        held = held + jnp.where(route == e, to_col(row), 0.0)
    pg_ref[...] = held

    total = ac[zh, zi]
    for i in range(1, nz):
        source = lax.rem(z + i, nz)
        remote(zs.at[0, 0], zr.at[source], z_send.at[0, 0], z_recv.at[source], other_core).wait_recv()
        total = total + zr[source].astype(F32)
    dg_ref[...] = total

    for q in range(n_chunks):
        for way in range(2):
            for s in range(hops(q, way)):
                ring(q, way, s).wait_send()
    for copy in (
        meta_copies + [w_pair] + w_z + w_x + w_relay + [w_core] + core_copies
        + list(x_copies.values()) + value_copies
    ):
        copy.wait_send()
    for h in range(H):
        for i in range(nzh):
            @pl.when(z != i * H + h)
            def _():
                z_copy(h, i).wait_send()


def body(grad_out, routing, probs, down_weight, gate_saved, up_saved):
    ny, n_dp = lax.axis_size("expert"), lax.axis_size("dp")
    nz = n_dp // (2 * NX)
    toks, width = grad_out.shape
    slots, hid = gate_saved.shape[1:]
    half = hid // 2
    nzh = nz // H
    chan = nzh * 2 * toks
    lanes = -(-chan // 128) * 128
    n_chunks = NX * H
    depth = ny // 2
    dma = pltpu.SemaphoreType.DMA
    vmem = pl.BlockSpec(memory_space=pltpu.VMEM)
    scratch = [
        pltpu.VMEM((NX, H, ny, toks, lanes), BF16),
        pltpu.VMEM((ny, 8, 128), F32),
        pltpu.VMEM((ny * toks, hid), F32),
        pltpu.VMEM((ny, toks, hid), F32),
        pltpu.VMEM((ny, toks, hid), F32),
        pltpu.VMEM((ny, toks, 128), F32),
        pltpu.VMEM((toks, hid), BF16),
        pltpu.VMEM((2, NX, H, nzh, 2 * toks, half), BF16),
        pltpu.VMEM((n_chunks, 2, nzh, toks, hid), F32),
        pltpu.VMEM((n_chunks, nzh, toks, hid), F32),
        pltpu.VMEM((H, NX - 1, nzh, toks, hid), BF16),
        pltpu.VMEM((H, NX - 1, nzh, toks, hid), BF16),
        pltpu.VMEM((H, nzh, toks, hid), BF16),
        pltpu.VMEM((nz, toks, hid), BF16),
        pltpu.VMEM((H, nzh, toks, hid), F32),
        pltpu.VMEM((ny, 8, 128), F32),
        pltpu.VMEM((ny, 8, 128), F32),
        dma((n_chunks, 2, depth)), dma((n_chunks, 2, depth)),
        dma((ny - 1,)), dma((ny - 1,)),
        dma((2,)), dma((2,)),
        dma((nz - 1,)), dma((nz - 1,)),
        dma((4,)), dma((4,)),
        dma((n_chunks,)), dma((n_chunks,)),
        dma((H, NX - 1)), dma((H, NX - 1)),
        dma((H, nzh)), dma((nz,)),
        dma((ny - 1,)), dma((ny - 1,)),
    ]
    return pl.pallas_call(
        functools.partial(kernel, (ny, nz)),
        out_shape=(
            jax.ShapeDtypeStruct(down_weight.shape, F32),
            jax.ShapeDtypeStruct(gate_saved.shape, BF16),
            jax.ShapeDtypeStruct(gate_saved.shape, BF16),
            jax.ShapeDtypeStruct(routing.shape, F32),
        ),
        in_specs=[vmem] * 6,
        out_specs=(vmem,) * 4,
        scratch_shapes=scratch,
        compiler_params=pltpu.CompilerParams(
            collective_id=0, has_side_effects=True, vmem_limit_bytes=48 * 1024 * 1024
        ),
    )(grad_out, routing, probs, down_weight, gate_saved, up_saved)


def solution(mesh):
    in_specs = (
        P(("dp", "expert"), None),
        P(("dp", "expert"), None),
        P(("dp", "expert"), None),
        P("dp", "expert"),
        P("dp", None, "expert"),
        P("dp", None, "expert"),
    )
    out_specs = (
        P("dp", "expert"),
        P("dp", None, "expert"),
        P("dp", None, "expert"),
        P(("dp", "expert"), None),
    )
    return jax.shard_map(body, mesh=mesh, in_specs=in_specs, out_specs=out_specs, check_vma=False)
```

```python
import functools

import jax
import jax.numpy as jnp
from jax import lax
from jax.experimental import pallas as pl
from jax.experimental.pallas import tpu as pltpu
from jax.sharding import PartitionSpec as P

FLIGHT = 2
NX = 4
H = 2
G = 3
F32 = jnp.float32
BF16 = jnp.bfloat16


def kernel(
    cfg,
    tok_in, route_in, prob_in, w_in, gate_in, up_in,
    dg_ref, gg_ref, ug_ref, pg_ref,
    tok_ref, route_ref, prob_ref, w_ref, gate_ref, up_ref, fetch,
    yb, meta, wt, gt, ut, pt, wo, wg, pb, cr, xs, xr, zs, zr, ac, vs, vr,
    y_send, y_recv, m_send, m_recv, wc_send, wc_recv, wf_send, wf_recv, wz_send, wz_recv, wx_send, wx_recv,
    c_send, c_recv, x_send, x_recv, z_send, z_recv, v_send, v_recv,
):
    ny, nz = cfg
    toks, width = tok_in.shape
    slots, hid = gate_in.shape[0], gate_in.shape[2]
    half = hid // 2
    nzh = nz // H
    chan = nzh * 2 * toks
    lanes = yb.shape[-1]
    n_chunks = NX * H

    d = lax.axis_index("dp")
    y = lax.axis_index("expert")
    x = lax.div(d, 2 * nz)
    z = lax.rem(lax.div(d, 2), nz)
    c = lax.rem(d, 2)
    expert0 = lax.div(y, ny // FLIGHT) == 0

    def at_x(i):
        return (lax.rem(x + i, NX) * nz + z) * 2 + c, y

    def at_z(zz):
        return (x * nz + zz) * 2 + c, y

    def at_y(i):
        return d, lax.rem(y + i, ny)

    other_core = ((x * nz + z) * 2 + (1 - c), y)

    def remote(src, dst, send, recv, to):
        return pltpu.make_async_remote_copy(
            src_ref=src, dst_ref=dst, send_sem=send, recv_sem=recv,
            device_id=to, device_id_type=pl.DeviceIdType.MESH,
        )

    fetched = {}
    pairs = (
        (tok_in, tok_ref), (route_in, route_ref), (prob_in, prob_ref), (w_in, w_ref),
        (gate_in, gate_ref), (up_in, up_ref),
    )
    for i, (src, dst) in enumerate(pairs):
        fetched[i] = pltpu.make_async_copy(src, dst, fetch.at[i])
        fetched[i].start()

    barrier = pltpu.get_barrier_semaphore()
    partners = [other_core]
    partners += [at_x(i) for i in range(1, NX)]
    partners += [at_z(lax.rem(z + i, nz)) for i in range(1, nz)]
    partners += [at_y(i) for i in range(1, ny)]
    for to in partners:
        pl.semaphore_signal(barrier, inc=1, device_id=to, device_id_type=pl.DeviceIdType.MESH)

    sub = lax.broadcasted_iota(jnp.int32, (toks, toks), 0)
    lane = lax.broadcasted_iota(jnp.int32, (toks, toks), 1)
    eye = sub == lane

    def to_row(col):
        return jnp.sum(jnp.where(eye, col, 0.0), axis=0, keepdims=True)

    def to_col(row):
        return jnp.sum(jnp.where(eye, row, 0.0), axis=1, keepdims=True)

    fetched[1].wait()
    fetched[2].wait()
    route = route_ref[...]
    prob = prob_ref[...].astype(F32)
    rows = []
    for e in range(FLIGHT):
        hit = route == e
        on = jnp.sum(jnp.where(hit, 1.0, 0.0), axis=0, keepdims=True)
        weight = jnp.sum(jnp.where(hit, prob, 0.0), axis=0, keepdims=True)
        before = jnp.sum(jnp.where(sub < lane, to_col(on), 0.0), axis=0, keepdims=True)
        rows += [weight, jnp.where(on > 0.0, before, -1.0)]
    line = lax.broadcasted_iota(jnp.int32, (8, toks), 0)
    tile = jnp.zeros((8, toks), F32)
    for i, row in enumerate(rows):
        tile = jnp.where(line == i, row, tile)
    meta[y] = jnp.zeros((8, 128), F32)
    meta[y, :, :toks] = tile

    def arrange(h):
        for k in range(NX):
            pieces = []
            for i in range(nzh):
                start = ((k * nz) + i * H + h) * 2 * toks
                pieces.append(tok_ref[:, start:start + 2 * toks].astype(F32))
            if lanes > chan:
                pieces.append(jnp.zeros((toks, lanes - chan), F32))
            yb[k, h, y] = jnp.concatenate(pieces, axis=1).astype(BF16)

    fetched[0].wait()
    arrange(0)
    pl.semaphore_wait(barrier, len(partners))

    def target_x(q):
        return lax.rem(x + 1 + q % NX, NX)

    def hops(q, way):
        return ny // 2 if (q + way) % 2 == 0 else ny // 2 - 1

    def ring(q, way, s):
        block = lax.rem(y + ny - s, ny) if way == 0 else lax.rem(y + s, ny)
        ref = yb.at[target_x(q), q // NX, block]
        return remote(
            ref, ref, y_send.at[q, way, s], y_recv.at[q, way, s], at_y(1 if way == 0 else ny - 1)
        )

    meta_copies = [
        remote(meta.at[y], meta.at[y], m_send.at[i - 1], m_recv.at[i - 1], at_y(i))
        for i in range(1, ny)
    ]
    w_pair = remote(w_ref, wo, wc_send.at[0], wc_recv.at[0], other_core)
    zh, zi = lax.rem(z, H), lax.div(z, H)
    w_own = wg.at[c, x, lax.rem(z, G), lax.div(z, G)]
    w_far = [
        remote(w_own, w_own, wf_send.at[i - 1], wf_recv.at[i - 1], at_z(lax.rem(z + i * G, nz)))
        for i in range(1, nz // G)
    ]
    w_class = wg.at[c, x, lax.rem(z, G)]
    w_near = [
        remote(w_class, w_class, wz_send.at[i], wz_recv.at[i], at_z(lax.rem(z + (1 if i == 0 else nz - 1), nz)))
        for i in range(2)
    ]
    w_x = [
        remote(wg.at[c, x], wg.at[c, x], wx_send.at[i], wx_recv.at[i], at_x(1 if i == 0 else NX - 1))
        for i in range(2)
    ]
    w_relay = []
    for i in range(2):
        ref = wg.at[c, lax.rem(x + (NX - 1 if i == 0 else 1), NX), :, pl.ds(i * (nz // G // 2), nz // G // 2)]
        w_relay.append(
            remote(ref, ref, wx_send.at[2 + i], wx_recv.at[2 + i], at_x(1 if i == 0 else NX - 1))
        )
    w_core = remote(wg.at[c], wg.at[c], wc_send.at[1], wc_recv.at[1], other_core)
    core_copies = [
        remote(pb.at[q, 1 - c], cr.at[q], c_send.at[q], c_recv.at[q], other_core)
        for q in range(n_chunks)
    ]
    x_copies = {
        q: remote(
            xs.at[q // NX, q % NX], xr.at[q // NX, q % NX],
            x_send.at[q // NX, q % NX], x_recv.at[q // NX, q % NX], at_x(1 + q % NX),
        )
        for q in range(n_chunks) if q % NX < NX - 1
    }
    value_copies = [
        remote(
            vs.at[lax.rem(y + i, ny)], vr.at[y], v_send.at[i - 1], v_recv.at[i - 1], at_y(i)
        )
        for i in range(1, ny)
    ]

    def z_copy(h, i):
        return remote(
            zs.at[h, i], zr.at[z], z_send.at[h, i], z_recv.at[z], at_z(i * H + h)
        )

    def row_of(source, field):
        both = meta[source][:, :toks]
        return jnp.where(expert0, both[field:field + 1], both[2 + field:3 + field])

    def spread():
        fetched[4].wait()
        fetched[5].wait()
        for copy in meta_copies:
            copy.wait_recv()
        tables = []
        for s in range(ny):
            slot_col = to_col(row_of(s, 1))
            p_col = to_col(row_of(s, 0))
            place = lax.broadcasted_iota(jnp.int32, (toks, slots * ny), 1)
            mine = (lax.rem(place, ny) == s) & (lax.div(place, ny).astype(F32) == slot_col)
            tables.append(jnp.where(mine, 1.0, 0.0))
            pt[pl.ds(s * toks, toks), :] = jnp.broadcast_to(p_col, (toks, 128))
        table = jnp.concatenate(tables, axis=0).astype(BF16)
        g = jnp.dot(table, saved(gate_ref), preferred_element_type=F32)
        u = jnp.dot(table, saved(up_ref), preferred_element_type=F32)
        gt[...] = g
        ut[...] = u
        hidden = g * jax.nn.sigmoid(g) * u
        wt[...] = (pt[:, :1] * hidden).astype(BF16)

    def saved(ref):
        return ref[...].astype(F32).reshape(slots * ny, hid).astype(BF16)

    def tokens_of(k, h):
        return yb[k, h].astype(F32).reshape(ny * toks, lanes).astype(BF16)

    def multiply(q):
        for way in range(2):
            if hops(q, way):
                ring(q, way, hops(q, way) - 1).wait_recv()
        part = lax.dot_general(
            tokens_of(target_x(q), q // NX), wt[...], (((0,), (0,)), ((), ())),
            preferred_element_type=F32,
        )
        for i in range(nzh):
            for j in range(2):
                lo = (i * 2 + j) * toks
                pb[q, j, i] = part[lo:lo + toks]
        core_copies[q].start()

    def pair(q):
        h, j = q // NX, q % NX
        core_copies[q].wait_recv()
        total = pb[q, c] + cr[q]
        if j < NX - 1:
            xs[h, j] = total.astype(BF16)
            x_copies[q].start()
            return
        for i in range(NX - 1):
            x_copies[h * NX + i].wait_recv()
            total = total + xr[h, i].astype(F32)
        ac[h] = total
        zs[h] = total.astype(BF16)
        for i in range(nzh):
            @pl.when(z != i * H + h)
            def _():
                z_copy(h, i).start()

    def w_first():
        w_pair.wait_recv()
        mine = w_ref[...].astype(F32)
        theirs = wo[...].astype(F32)
        first = jnp.where(c == 0, mine, theirs)
        second = jnp.where(c == 0, theirs, mine)
        both = jnp.concatenate([first, second], axis=0)
        wg[c, x, lax.rem(z, G), lax.div(z, G)] = jnp.where(c == 0, both[:, :half], both[:, half:]).astype(BF16)
        for copy in w_far:
            copy.start()

    def w_near_step():
        for copy in w_far:
            copy.wait_recv()
        for copy in w_near:
            copy.start()

    def w_second():
        for copy in w_near:
            copy.wait_recv()
        for copy in w_x:
            copy.start()

    def w_third():
        for copy, relay in zip(w_x, w_relay):
            copy.wait_recv()
            relay.start()

    def w_fourth():
        for relay in w_relay:
            relay.wait_recv()
        w_core.start()

    def activations():
        w_core.wait_recv()
        dh = jnp.zeros((ny * toks, hid), F32)
        for k in range(NX):
            for h in range(H):
                weights = jnp.concatenate(
                    [
                        jnp.concatenate(
                            [wg[i, k, zz % G, zz // G] for zz in range(h, nz, H)], axis=0
                        )
                        for i in range(2)
                    ],
                    axis=1,
                )
                dh = dh + jnp.dot(
                    tokens_of(k, h)[:, :chan], weights, preferred_element_type=F32
                )
        g, u, p = gt[...], ut[...], pt[:, :1]
        sig = jax.nn.sigmoid(g)
        act = g * sig
        hidden = act * u
        scaled = p * dh
        up_tok = (scaled * act).astype(BF16)
        gate_tok = (scaled * u * sig * (1.0 + g * (1.0 - sig))).astype(BF16)
        value = jnp.sum(hidden * dh, axis=1, keepdims=True)
        for s in range(ny):
            row = to_row(value[s * toks:(s + 1) * toks])
            vs[s, :, :toks] = jnp.broadcast_to(row, (8, toks))
        for copy in value_copies:
            copy.start()
        vr[y] = vs[y]
        packs = []
        for s in range(ny):
            place = lax.broadcasted_iota(jnp.int32, (slots * ny, toks), 0)
            mine = (lax.rem(place, ny) == s) & (lax.div(place, ny).astype(F32) == row_of(s, 1))
            packs.append(jnp.where(mine, 1.0, 0.0))
        pack = jnp.concatenate(packs, axis=1).astype(BF16)
        for ref, values in ((ug_ref, up_tok), (gg_ref, gate_tok)):
            packed = jnp.dot(pack, values, preferred_element_type=F32)
            ref[...] = packed.reshape(slots, ny, hid).astype(BF16)

    fetched[3].wait()
    w_pair.start()
    for copy in meta_copies:
        copy.start()
    depth = ny // 2
    for way in range(2):
        if hops(0, way):
            ring(0, way, 0).start()
    arrange(1)
    for t in range(n_chunks + depth + 1):
        if t + 1 < n_chunks:
            for way in range(2):
                if hops(t + 1, way):
                    ring(t + 1, way, 0).start()
        for s in range(1, depth):
            q = t - s
            if 0 <= q < n_chunks:
                for way in range(2):
                    if s < hops(q, way):
                        ring(q, way, s - 1).wait_recv()
                        ring(q, way, s).start()
        if t == 0:
            w_first()
            spread()
        if t == 2:
            w_near_step()
        if t == 4:
            w_second()
        if t == 6:
            w_third()
        if t == 7:
            w_fourth()
        q = t - depth
        if 0 <= q < n_chunks:
            multiply(q)
        q = t - depth - 1
        if 0 <= q < n_chunks:
            pair(q)
    activations()

    for copy in value_copies:
        copy.wait_recv()
    held = jnp.zeros(route.shape, F32)
    share = ny // FLIGHT
    for e in range(FLIGHT):
        row = vr[e * share][0:1, :toks]
        for i in range(1, share):
            row = row + vr[e * share + i][0:1, :toks]
        held = held + jnp.where(route == e, row, 0.0)
    pg_ref[...] = held

    total = ac[zh, zi]
    for i in range(1, nz):
        source = lax.rem(z + i, nz)
        remote(zs.at[0, 0], zr.at[source], z_send.at[0, 0], z_recv.at[source], other_core).wait_recv()
        total = total + zr[source].astype(F32)
    dg_ref[...] = total

    for q in range(n_chunks):
        for way in range(2):
            for s in range(hops(q, way)):
                ring(q, way, s).wait_send()
    for copy in (
        meta_copies + [w_pair] + w_far + w_near + w_x + w_relay + [w_core] + core_copies
        + list(x_copies.values()) + value_copies
    ):
        copy.wait_send()
    for h in range(H):
        for i in range(nzh):
            @pl.when(z != i * H + h)
            def _():
                z_copy(h, i).wait_send()


def hand_over(a, b, c, d, a_out, b_out, c_out, d_out, sem):
    copies = [
        pltpu.make_async_copy(src, dst, sem.at[i])
        for i, (src, dst) in enumerate(((a, a_out), (b, b_out), (c, c_out), (d, d_out)))
    ]
    for copy in copies:
        copy.start()
    for copy in copies:
        copy.wait()


def body(grad_out, routing, probs, down_weight, gate_saved, up_saved):
    ny, n_dp = lax.axis_size("expert"), lax.axis_size("dp")
    nz = n_dp // (2 * NX)
    toks, width = grad_out.shape
    slots, hid = gate_saved.shape[1:]
    saved = (slots, ny, hid)
    top = routing.shape[1]
    half = hid // 2
    nzh = nz // H
    chan = nzh * 2 * toks
    lanes = -(-chan // 128) * 128
    n_chunks = NX * H
    depth = ny // 2
    dma = pltpu.SemaphoreType.DMA
    vmem = pl.BlockSpec(memory_space=pltpu.VMEM)
    scratch = [
        pltpu.VMEM(grad_out.shape, BF16),
        pltpu.VMEM((top, toks), jnp.int32),
        pltpu.VMEM((top, toks), BF16),
        pltpu.VMEM(down_weight.shape, BF16),
        pltpu.VMEM(saved, BF16),
        pltpu.VMEM(saved, BF16),
        dma((6,)),
        pltpu.VMEM((NX, H, ny, toks, lanes), BF16),
        pltpu.VMEM((ny, 8, 128), F32),
        pltpu.VMEM((ny * toks, hid), BF16),
        pltpu.VMEM((ny * toks, hid), F32),
        pltpu.VMEM((ny * toks, hid), F32),
        pltpu.VMEM((ny * toks, 128), F32),
        pltpu.VMEM((toks, hid), BF16),
        pltpu.VMEM((2, NX, G, nz // G, 2 * toks, half), BF16),
        pltpu.VMEM((n_chunks, 2, nzh, toks, hid), F32),
        pltpu.VMEM((n_chunks, nzh, toks, hid), F32),
        pltpu.VMEM((H, NX - 1, nzh, toks, hid), BF16),
        pltpu.VMEM((H, NX - 1, nzh, toks, hid), BF16),
        pltpu.VMEM((H, nzh, toks, hid), BF16),
        pltpu.VMEM((nz, toks, hid), BF16),
        pltpu.VMEM((H, nzh, toks, hid), F32),
        pltpu.VMEM((ny, 8, 128), F32),
        pltpu.VMEM((ny, 8, 128), F32),
        dma((n_chunks, 2, depth)), dma((n_chunks, 2, depth)),
        dma((ny - 1,)), dma((ny - 1,)),
        dma((2,)), dma((2,)),
        dma((nz // G - 1,)), dma((nz // G - 1,)),
        dma((2,)), dma((2,)),
        dma((4,)), dma((4,)),
        dma((n_chunks,)), dma((n_chunks,)),
        dma((H, NX - 1)), dma((H, NX - 1)),
        dma((H, nzh)), dma((nz,)),
        dma((ny - 1,)), dma((ny - 1,)),
    ]
    shapes = (
        jax.ShapeDtypeStruct(down_weight.shape, F32),
        jax.ShapeDtypeStruct(saved, BF16),
        jax.ShapeDtypeStruct(saved, BF16),
        jax.ShapeDtypeStruct((top, toks), F32),
    )
    parts = pl.pallas_call(
        functools.partial(kernel, (ny, nz)),
        out_shape=shapes,
        in_specs=[pl.BlockSpec(memory_space=pl.ANY)] * 6,
        out_specs=(vmem,) * 4,
        scratch_shapes=scratch,
        compiler_params=pltpu.CompilerParams(
            collective_id=0, has_side_effects=True, vmem_limit_bytes=63 * 1024 * 1024
        ),
    )(
        grad_out, routing.T, probs.T, down_weight,
        jnp.transpose(gate_saved, (1, 0, 2)), jnp.transpose(up_saved, (1, 0, 2)),
    )
    down_grad, gate_grad, up_grad, prob_grad = pl.pallas_call(
        hand_over,
        out_shape=shapes,
        in_specs=[pl.BlockSpec(memory_space=pl.ANY)] * 4,
        out_specs=(pl.BlockSpec(memory_space=pl.ANY),) * 4,
        scratch_shapes=[dma((4,))],
        compiler_params=pltpu.CompilerParams(vmem_limit_bytes=63 * 1024 * 1024),
    )(*parts)
    return (
        down_grad, jnp.transpose(gate_grad, (1, 0, 2)), jnp.transpose(up_grad, (1, 0, 2)),
        prob_grad.T,
    )


def solution(mesh):
    in_specs = (
        P(("dp", "expert"), None),
        P(("dp", "expert"), None),
        P(("dp", "expert"), None),
        P("dp", "expert"),
        P("dp", None, "expert"),
        P("dp", None, "expert"),
    )
    out_specs = (
        P("dp", "expert"),
        P("dp", None, "expert"),
        P("dp", None, "expert"),
        P(("dp", "expert"), None),
    )
    return jax.shard_map(body, mesh=mesh, in_specs=in_specs, out_specs=out_specs, check_vma=False)
```

```python
import functools

import jax
import jax.numpy as jnp
from jax import lax
from jax.experimental import pallas as pl
from jax.experimental.pallas import tpu as pltpu
from jax.sharding import PartitionSpec as P

FLIGHT = 2
NX = 4
H = 2
G = 3
SKEW = 2
AHEAD = 3
LAG = 2
WAIT_X = 2
SPREAD = 2
W_SLOTS = (1, 4, 6, 9, 11)
F32 = jnp.float32
BF16 = jnp.bfloat16


def kernel(
    cfg,
    tok_in, route_in, prob_in, w_in, gate_in, up_in,
    dg_ref, gg_ref, ug_ref, pg_ref,
    tok_ref, route_ref, prob_ref, w_ref, gate_ref, up_ref, fetch,
    yb, meta, wt, gt, ut, pt, wo, wg, pb, cr, xs, xr, zs, zr, ac, vs, vr,
    y_send, y_recv, m_send, m_recv, wc_send, wc_recv, wf_send, wf_recv, wz_send, wz_recv, wx_send, wx_recv,
    c_send, c_recv, x_send, x_recv, z_send, z_recv, v_send, v_recv,
):
    ny, nz = cfg
    toks, width = tok_in.shape
    slots, hid = gate_in.shape[0], gate_in.shape[2]
    half = hid // 2
    nzh = nz // H
    chan = nzh * 2 * toks
    lanes = yb.shape[-1]
    n_chunks = NX * H

    d = lax.axis_index("dp")
    y = lax.axis_index("expert")
    x = lax.div(d, 2 * nz)
    z = lax.rem(lax.div(d, 2), nz)
    c = lax.rem(d, 2)
    expert0 = lax.div(y, ny // FLIGHT) == 0

    def at_x(i):
        return (lax.rem(x + i, NX) * nz + z) * 2 + c, y

    def at_z(zz):
        return (x * nz + zz) * 2 + c, y

    def at_y(i):
        return d, lax.rem(y + i, ny)

    other_core = ((x * nz + z) * 2 + (1 - c), y)

    def remote(src, dst, send, recv, to):
        return pltpu.make_async_remote_copy(
            src_ref=src, dst_ref=dst, send_sem=send, recv_sem=recv,
            device_id=to, device_id_type=pl.DeviceIdType.MESH,
        )

    fetched = {}
    pairs = (
        (tok_in, tok_ref), (route_in, route_ref), (prob_in, prob_ref), (w_in, w_ref),
        (gate_in, gate_ref), (up_in, up_ref),
    )
    for i, (src, dst) in enumerate(pairs):
        fetched[i] = pltpu.make_async_copy(src, dst, fetch.at[i])
        fetched[i].start()

    barrier = pltpu.get_barrier_semaphore()
    partners = [other_core]
    partners += [at_x(i) for i in range(1, NX)]
    partners += [at_z(lax.rem(z + i, nz)) for i in range(1, nz)]
    partners += [at_y(i) for i in range(1, ny)]
    for to in partners:
        pl.semaphore_signal(barrier, inc=1, device_id=to, device_id_type=pl.DeviceIdType.MESH)

    sub = lax.broadcasted_iota(jnp.int32, (toks, toks), 0)
    lane = lax.broadcasted_iota(jnp.int32, (toks, toks), 1)
    eye = sub == lane

    def to_row(col):
        return jnp.sum(jnp.where(eye, col, 0.0), axis=0, keepdims=True)

    def to_col(row):
        return jnp.sum(jnp.where(eye, row, 0.0), axis=1, keepdims=True)

    fetched[1].wait()
    fetched[2].wait()
    route = route_ref[...]
    prob = prob_ref[...].astype(F32)
    rows = []
    for e in range(FLIGHT):
        hit = route == e
        on = jnp.sum(jnp.where(hit, 1.0, 0.0), axis=0, keepdims=True)
        weight = jnp.sum(jnp.where(hit, prob, 0.0), axis=0, keepdims=True)
        before = jnp.sum(jnp.where(sub < lane, to_col(on), 0.0), axis=0, keepdims=True)
        rows += [weight, jnp.where(on > 0.0, before, -1.0)]
    line = lax.broadcasted_iota(jnp.int32, (8, toks), 0)
    tile = jnp.zeros((8, toks), F32)
    for i, row in enumerate(rows):
        tile = jnp.where(line == i, row, tile)
    meta[y] = jnp.zeros((8, 128), F32)
    meta[y, :, :toks] = tile

    def arrange(h):
        for k in range(NX):
            pieces = []
            for i in range(nzh):
                start = ((k * nz) + i * H + h) * 2 * toks
                pieces.append(tok_ref[:, start:start + 2 * toks].astype(F32))
            if lanes > chan:
                pieces.append(jnp.zeros((toks, lanes - chan), F32))
            yb[k, h, y] = jnp.concatenate(pieces, axis=1).astype(BF16)

    fetched[0].wait()
    arrange(0)
    pl.semaphore_wait(barrier, len(partners))

    def target_x(q):
        return lax.rem(x + 1 + q % NX, NX)

    def hops(q, way):
        return ny // 2 if (q + way) % 2 == 0 else ny // 2 - 1

    def ring(q, way, s):
        block = lax.rem(y + ny - s, ny) if way == 0 else lax.rem(y + s, ny)
        ref = yb.at[target_x(q), q // NX, block]
        return remote(
            ref, ref, y_send.at[q, way, s], y_recv.at[q, way, s], at_y(1 if way == 0 else ny - 1)
        )

    meta_copies = [
        remote(meta.at[y], meta.at[y], m_send.at[i - 1], m_recv.at[i - 1], at_y(i))
        for i in range(1, ny)
    ]
    w_pair = remote(w_ref, wo, wc_send.at[0], wc_recv.at[0], other_core)
    zh, zi = lax.rem(z, H), lax.div(z, H)
    w_own = wg.at[c, x, lax.rem(z, G), lax.div(z, G)]
    w_far = [
        remote(w_own, w_own, wf_send.at[i - 1], wf_recv.at[i - 1], at_z(lax.rem(z + i * G, nz)))
        for i in range(1, nz // G)
    ]
    w_class = wg.at[c, x, lax.rem(z, G)]
    w_near = [
        remote(w_class, w_class, wz_send.at[i], wz_recv.at[i], at_z(lax.rem(z + (1 if i == 0 else nz - 1), nz)))
        for i in range(2)
    ]
    w_x = [
        remote(wg.at[c, x], wg.at[c, x], wx_send.at[i], wx_recv.at[i], at_x(1 if i == 0 else NX - 1))
        for i in range(2)
    ]
    w_relay = []
    for i in range(2):
        ref = wg.at[c, lax.rem(x + (NX - 1 if i == 0 else 1), NX), :, pl.ds(i * (nz // G // 2), nz // G // 2)]
        w_relay.append(
            remote(ref, ref, wx_send.at[2 + i], wx_recv.at[2 + i], at_x(1 if i == 0 else NX - 1))
        )
    w_core = remote(wg.at[c], wg.at[c], wc_send.at[1], wc_recv.at[1], other_core)
    core_copies = [
        remote(pb.at[q, 1 - c], cr.at[q], c_send.at[q], c_recv.at[q], other_core)
        for q in range(n_chunks)
    ]
    x_copies = {
        q: remote(
            xs.at[q // NX, q % NX], xr.at[q // NX, q % NX],
            x_send.at[q // NX, q % NX], x_recv.at[q // NX, q % NX], at_x(1 + q % NX),
        )
        for q in range(n_chunks) if q % NX < NX - 1
    }
    value_copies = [
        remote(
            vs.at[lax.rem(y + i, ny)], vr.at[y], v_send.at[i - 1], v_recv.at[i - 1], at_y(i)
        )
        for i in range(1, ny)
    ]

    def z_copy(h, i):
        return remote(
            zs.at[h, i], zr.at[z], z_send.at[h, i], z_recv.at[z], at_z(i * H + h)
        )

    def row_of(source, field):
        both = meta[source][:, :toks]
        return jnp.where(expert0, both[field:field + 1], both[2 + field:3 + field])

    def spread():
        fetched[4].wait()
        fetched[5].wait()
        for copy in meta_copies:
            copy.wait_recv()
        tables = []
        for s in range(ny):
            slot_col = to_col(row_of(s, 1))
            p_col = to_col(row_of(s, 0))
            place = lax.broadcasted_iota(jnp.int32, (toks, slots * ny), 1)
            mine = (lax.rem(place, ny) == s) & (lax.div(place, ny).astype(F32) == slot_col)
            tables.append(jnp.where(mine, 1.0, 0.0))
            pt[pl.ds(s * toks, toks), :] = jnp.broadcast_to(p_col, (toks, 128))
        table = jnp.concatenate(tables, axis=0).astype(BF16)
        g = jnp.dot(table, saved(gate_ref), preferred_element_type=F32)
        u = jnp.dot(table, saved(up_ref), preferred_element_type=F32)
        gt[...] = g
        ut[...] = u
        hidden = g * jax.nn.sigmoid(g) * u
        wt[...] = (pt[:, :1] * hidden).astype(BF16)

    def saved(ref):
        return ref[...].astype(F32).reshape(slots * ny, hid).astype(BF16)

    def tokens_of(k, h):
        return yb[k, h].astype(F32).reshape(ny * toks, lanes).astype(BF16)

    def multiply(q):
        for way in range(2):
            if hops(q, way):
                ring(q, way, hops(q, way) - 1).wait_recv()
        part = lax.dot_general(
            tokens_of(target_x(q), q // NX), wt[...], (((0,), (0,)), ((), ())),
            preferred_element_type=F32,
        )
        for i in range(nzh):
            for j in range(2):
                lo = (i * 2 + j) * toks
                pb[q, j, i] = part[lo:lo + toks]
        core_copies[q].start()

    def pair(q):
        h, j = q // NX, q % NX
        core_copies[q].wait_recv()
        total = pb[q, c] + cr[q]
        if j < NX - 1:
            xs[h, j] = total.astype(BF16)
            x_copies[q].start()
        else:
            ac[h] = total

    def finish(h):
        total = ac[h]
        for i in range(NX - 1):
            x_copies[h * NX + i].wait_recv()
            total = total + xr[h, i].astype(F32)
        ac[h] = total
        zs[h] = total.astype(BF16)
        for i in range(nzh):
            @pl.when(z != i * H + h)
            def _():
                z_copy(h, i).start()

    def w_first():
        w_pair.wait_recv()
        mine = w_ref[...].astype(F32)
        theirs = wo[...].astype(F32)
        first = jnp.where(c == 0, mine, theirs)
        second = jnp.where(c == 0, theirs, mine)
        both = jnp.concatenate([first, second], axis=0)
        wg[c, x, lax.rem(z, G), lax.div(z, G)] = jnp.where(c == 0, both[:, :half], both[:, half:]).astype(BF16)
        for copy in w_far:
            copy.start()

    def w_near_step():
        for copy in w_far:
            copy.wait_recv()
        for copy in w_near:
            copy.start()

    def w_second():
        for copy in w_near:
            copy.wait_recv()
        for copy in w_x:
            copy.start()

    def w_third():
        for copy, relay in zip(w_x, w_relay):
            copy.wait_recv()
            relay.start()

    def w_fourth():
        for relay in w_relay:
            relay.wait_recv()
        w_core.start()

    def activations():
        w_core.wait_recv()
        dh = jnp.zeros((ny * toks, hid), F32)
        for k in range(NX):
            for h in range(H):
                weights = jnp.concatenate(
                    [
                        jnp.concatenate(
                            [wg[i, k, zz % G, zz // G] for zz in range(h, nz, H)], axis=0
                        )
                        for i in range(2)
                    ],
                    axis=1,
                )
                dh = dh + jnp.dot(
                    tokens_of(k, h)[:, :chan], weights, preferred_element_type=F32
                )
        g, u, p = gt[...], ut[...], pt[:, :1]
        sig = jax.nn.sigmoid(g)
        act = g * sig
        hidden = act * u
        scaled = p * dh
        up_tok = (scaled * act).astype(BF16)
        gate_tok = (scaled * u * sig * (1.0 + g * (1.0 - sig))).astype(BF16)
        value = jnp.sum(hidden * dh, axis=1, keepdims=True)
        for s in range(ny):
            row = to_row(value[s * toks:(s + 1) * toks])
            vs[s, :, :toks] = jnp.broadcast_to(row, (8, toks))
        for copy in value_copies:
            copy.start()
        vr[y] = vs[y]
        packs = []
        for s in range(ny):
            place = lax.broadcasted_iota(jnp.int32, (slots * ny, toks), 0)
            mine = (lax.rem(place, ny) == s) & (lax.div(place, ny).astype(F32) == row_of(s, 1))
            packs.append(jnp.where(mine, 1.0, 0.0))
        pack = jnp.concatenate(packs, axis=1).astype(BF16)
        for ref, values in ((ug_ref, up_tok), (gg_ref, gate_tok)):
            packed = jnp.dot(pack, values, preferred_element_type=F32)
            ref[...] = packed.reshape(slots, ny, hid).astype(BF16)

    fetched[3].wait()
    w_pair.start()
    depth = ny // 2
    work = {0: [lambda: arrange(1)], SPREAD: [spread]}
    for slot, step in zip(W_SLOTS, (w_first, w_near_step, w_second, w_third, w_fourth)):
        work.setdefault(slot, []).append(step)
    last = n_chunks - 1 + SKEW * (depth - 1) + LAG
    for t in range(last + 1):
        for q in range(n_chunks):
            if max(0, q - AHEAD) == t:
                for way in range(2):
                    if hops(q, way):
                        ring(q, way, 0).start()
        if t == 0:
            for copy in meta_copies:
                copy.start()
        for s in range(1, depth):
            q = t - SKEW * (s - 1)
            if 0 <= q < n_chunks:
                for way in range(2):
                    if s < hops(q, way):
                        ring(q, way, s - 1).wait_recv()
                        ring(q, way, s).start()
        for step in work.get(t, []):
            step()
        q = t - SKEW * (depth - 1)
        if 0 <= q < n_chunks:
            multiply(q)
        q = t - SKEW * (depth - 1) - LAG
        if 0 <= q < n_chunks:
            if q == n_chunks - 1:
                activations()
            pair(q)
        if t == NX - 1 + SKEW * (depth - 1) + LAG + WAIT_X:
            finish(0)
    finish(1)

    for copy in value_copies:
        copy.wait_recv()
    held = jnp.zeros(route.shape, F32)
    share = ny // FLIGHT
    for e in range(FLIGHT):
        row = vr[e * share][0:1, :toks]
        for i in range(1, share):
            row = row + vr[e * share + i][0:1, :toks]
        held = held + jnp.where(route == e, row, 0.0)
    pg_ref[...] = held

    total = ac[zh, zi]
    for i in range(1, nz):
        source = lax.rem(z + i, nz)
        remote(zs.at[0, 0], zr.at[source], z_send.at[0, 0], z_recv.at[source], other_core).wait_recv()
        total = total + zr[source].astype(F32)
    dg_ref[...] = total

    for q in range(n_chunks):
        for way in range(2):
            for s in range(hops(q, way)):
                ring(q, way, s).wait_send()
    for copy in (
        meta_copies + [w_pair] + w_far + w_near + w_x + w_relay + [w_core] + core_copies
        + list(x_copies.values()) + value_copies
    ):
        copy.wait_send()
    for h in range(H):
        for i in range(nzh):
            @pl.when(z != i * H + h)
            def _():
                z_copy(h, i).wait_send()


def hand_over(a, b, c, d, a_out, b_out, c_out, d_out):
    for src, dst in ((a, a_out), (b, b_out), (c, c_out), (d, d_out)):
        dst[...] = src[...]


def body(grad_out, routing, probs, down_weight, gate_saved, up_saved):
    ny, n_dp = lax.axis_size("expert"), lax.axis_size("dp")
    nz = n_dp // (2 * NX)
    toks, width = grad_out.shape
    slots, hid = gate_saved.shape[1:]
    saved = (slots, ny, hid)
    top = routing.shape[1]
    half = hid // 2
    nzh = nz // H
    chan = nzh * 2 * toks
    lanes = -(-chan // 128) * 128
    n_chunks = NX * H
    depth = ny // 2
    dma = pltpu.SemaphoreType.DMA
    vmem = pl.BlockSpec(memory_space=pltpu.VMEM)
    scratch = [
        pltpu.VMEM(grad_out.shape, BF16),
        pltpu.VMEM((top, toks), jnp.int32),
        pltpu.VMEM((top, toks), BF16),
        pltpu.VMEM(down_weight.shape, BF16),
        pltpu.VMEM(saved, BF16),
        pltpu.VMEM(saved, BF16),
        dma((6,)),
        pltpu.VMEM((NX, H, ny, toks, lanes), BF16),
        pltpu.VMEM((ny, 8, 128), F32),
        pltpu.VMEM((ny * toks, hid), BF16),
        pltpu.VMEM((ny * toks, hid), F32),
        pltpu.VMEM((ny * toks, hid), F32),
        pltpu.VMEM((ny * toks, 128), F32),
        pltpu.VMEM((toks, hid), BF16),
        pltpu.VMEM((2, NX, G, nz // G, 2 * toks, half), BF16),
        pltpu.VMEM((n_chunks, 2, nzh, toks, hid), F32),
        pltpu.VMEM((n_chunks, nzh, toks, hid), F32),
        pltpu.VMEM((H, NX - 1, nzh, toks, hid), BF16),
        pltpu.VMEM((H, NX - 1, nzh, toks, hid), BF16),
        pltpu.VMEM((H, nzh, toks, hid), BF16),
        pltpu.VMEM((nz, toks, hid), BF16),
        pltpu.VMEM((H, nzh, toks, hid), F32),
        pltpu.VMEM((ny, 8, 128), F32),
        pltpu.VMEM((ny, 8, 128), F32),
        dma((n_chunks, 2, depth)), dma((n_chunks, 2, depth)),
        dma((ny - 1,)), dma((ny - 1,)),
        dma((2,)), dma((2,)),
        dma((nz // G - 1,)), dma((nz // G - 1,)),
        dma((2,)), dma((2,)),
        dma((4,)), dma((4,)),
        dma((n_chunks,)), dma((n_chunks,)),
        dma((H, NX - 1)), dma((H, NX - 1)),
        dma((H, nzh)), dma((nz,)),
        dma((ny - 1,)), dma((ny - 1,)),
    ]
    shapes = (
        jax.ShapeDtypeStruct(down_weight.shape, F32),
        jax.ShapeDtypeStruct(saved, BF16),
        jax.ShapeDtypeStruct(saved, BF16),
        jax.ShapeDtypeStruct((top, toks), F32),
    )
    parts = pl.pallas_call(
        functools.partial(kernel, (ny, nz)),
        out_shape=shapes,
        in_specs=[pl.BlockSpec(memory_space=pl.ANY)] * 6,
        out_specs=(vmem,) * 4,
        scratch_shapes=scratch,
        compiler_params=pltpu.CompilerParams(
            collective_id=0, has_side_effects=True, vmem_limit_bytes=63 * 1024 * 1024
        ),
    )(
        grad_out, routing.T, probs.T, down_weight,
        jnp.transpose(gate_saved, (1, 0, 2)), jnp.transpose(up_saved, (1, 0, 2)),
    )
    down_grad, gate_grad, up_grad, prob_grad = pl.pallas_call(
        hand_over,
        out_shape=shapes,
        in_specs=[vmem] * 4,
        out_specs=(vmem,) * 4,
        compiler_params=pltpu.CompilerParams(vmem_limit_bytes=63 * 1024 * 1024),
    )(*parts)
    return (
        down_grad, jnp.transpose(gate_grad, (1, 0, 2)), jnp.transpose(up_grad, (1, 0, 2)),
        prob_grad.T,
    )


def solution(mesh):
    in_specs = (
        P(("dp", "expert"), None),
        P(("dp", "expert"), None),
        P(("dp", "expert"), None),
        P("dp", "expert"),
        P("dp", None, "expert"),
        P("dp", None, "expert"),
    )
    out_specs = (
        P("dp", "expert"),
        P("dp", None, "expert"),
        P("dp", None, "expert"),
        P(("dp", "expert"), None),
    )
    return jax.shard_map(body, mesh=mesh, in_specs=in_specs, out_specs=out_specs, check_vma=False)
```

```python
import functools

import jax
import jax.numpy as jnp
from jax import lax
from jax.experimental import pallas as pl
from jax.experimental.pallas import tpu as pltpu
from jax.sharding import PartitionSpec as P

FLIGHT = 2
NX = 4
H = 4
G = 3
SKEW = 3
AHEAD = 5
LAG = 3
WAIT_X = 4
SPREAD = 4
W_SLOTS = (2, 8, 12, 17, 21)
F32 = jnp.float32
BF16 = jnp.bfloat16


def kernel(
    cfg,
    tok_in, route_in, prob_in, w_in, gate_in, up_in,
    dg_ref, gg_ref, ug_ref, pg_ref,
    tok_ref, route_ref, prob_ref, w_ref, gate_ref, up_ref, fetch,
    yb, meta, wt, gt, ut, pt, wo, wg, pb, cr, xs, xr, zs, zr, ac, vs, vr,
    y_send, y_recv, m_send, m_recv, wc_send, wc_recv, wf_send, wf_recv, wz_send, wz_recv, wx_send, wx_recv,
    c_send, c_recv, x_send, x_recv, z_send, z_recv, v_send, v_recv,
):
    ny, nz = cfg
    toks, width = tok_in.shape
    slots, hid = gate_in.shape[0], gate_in.shape[2]
    half = hid // 2
    nzh = nz // H
    chan = nzh * 2 * toks
    lanes = yb.shape[-1]
    n_chunks = NX * H

    d = lax.axis_index("dp")
    y = lax.axis_index("expert")
    x = lax.div(d, 2 * nz)
    z = lax.rem(lax.div(d, 2), nz)
    c = lax.rem(d, 2)
    expert0 = lax.div(y, ny // FLIGHT) == 0

    def at_x(i):
        return (lax.rem(x + i, NX) * nz + z) * 2 + c, y

    def at_z(zz):
        return (x * nz + zz) * 2 + c, y

    def at_y(i):
        return d, lax.rem(y + i, ny)

    other_core = ((x * nz + z) * 2 + (1 - c), y)

    def remote(src, dst, send, recv, to):
        return pltpu.make_async_remote_copy(
            src_ref=src, dst_ref=dst, send_sem=send, recv_sem=recv,
            device_id=to, device_id_type=pl.DeviceIdType.MESH,
        )

    fetched = {}
    pairs = (
        (tok_in, tok_ref), (route_in, route_ref), (prob_in, prob_ref), (w_in, w_ref),
        (gate_in, gate_ref), (up_in, up_ref),
    )
    for i, (src, dst) in enumerate(pairs):
        fetched[i] = pltpu.make_async_copy(src, dst, fetch.at[i])
        fetched[i].start()

    barrier = pltpu.get_barrier_semaphore()
    partners = [other_core]
    partners += [at_x(i) for i in range(1, NX)]
    partners += [at_z(lax.rem(z + i, nz)) for i in range(1, nz)]
    partners += [at_y(i) for i in range(1, ny)]
    for to in partners:
        pl.semaphore_signal(barrier, inc=1, device_id=to, device_id_type=pl.DeviceIdType.MESH)

    sub = lax.broadcasted_iota(jnp.int32, (toks, toks), 0)
    lane = lax.broadcasted_iota(jnp.int32, (toks, toks), 1)
    eye = sub == lane

    def to_row(col):
        return jnp.sum(jnp.where(eye, col, 0.0), axis=0, keepdims=True)

    def to_col(row):
        return jnp.sum(jnp.where(eye, row, 0.0), axis=1, keepdims=True)

    fetched[1].wait()
    fetched[2].wait()
    route = route_ref[...]
    prob = prob_ref[...].astype(F32)
    rows = []
    for e in range(FLIGHT):
        hit = route == e
        on = jnp.sum(jnp.where(hit, 1.0, 0.0), axis=0, keepdims=True)
        weight = jnp.sum(jnp.where(hit, prob, 0.0), axis=0, keepdims=True)
        before = jnp.sum(jnp.where(sub < lane, to_col(on), 0.0), axis=0, keepdims=True)
        rows += [weight, jnp.where(on > 0.0, before, -1.0)]
    line = lax.broadcasted_iota(jnp.int32, (8, toks), 0)
    tile = jnp.zeros((8, toks), F32)
    for i, row in enumerate(rows):
        tile = jnp.where(line == i, row, tile)
    meta[y] = jnp.zeros((8, 128), F32)
    meta[y, :, :toks] = tile

    def arrange(h):
        for k in range(NX):
            pieces = []
            for i in range(nzh):
                start = ((k * nz) + i * H + h) * 2 * toks
                pieces.append(tok_ref[:, start:start + 2 * toks].astype(F32))
            if lanes > chan:
                pieces.append(jnp.zeros((toks, lanes - chan), F32))
            yb[k, h, y] = jnp.concatenate(pieces, axis=1).astype(BF16)

    fetched[0].wait()
    for h in range(H):
        arrange(h)
    pl.semaphore_wait(barrier, len(partners))

    def target_x(q):
        return lax.rem(x + 1 + q % NX, NX)

    def hops(q, way):
        return ny // 2 if (q + way) % 2 == 0 else ny // 2 - 1

    def ring(q, way, s):
        block = lax.rem(y + ny - s, ny) if way == 0 else lax.rem(y + s, ny)
        ref = yb.at[target_x(q), q // NX, block]
        return remote(
            ref, ref, y_send.at[q, way, s], y_recv.at[q, way, s], at_y(1 if way == 0 else ny - 1)
        )

    meta_copies = [
        remote(meta.at[y], meta.at[y], m_send.at[i - 1], m_recv.at[i - 1], at_y(i))
        for i in range(1, ny)
    ]
    w_pair = remote(w_ref, wo, wc_send.at[0], wc_recv.at[0], other_core)
    zh, zi = lax.rem(z, H), lax.div(z, H)
    w_own = wg.at[c, x, lax.rem(z, G), lax.div(z, G)]
    w_far = [
        remote(w_own, w_own, wf_send.at[i - 1], wf_recv.at[i - 1], at_z(lax.rem(z + i * G, nz)))
        for i in range(1, nz // G)
    ]
    w_class = wg.at[c, x, lax.rem(z, G)]
    w_near = [
        remote(w_class, w_class, wz_send.at[i], wz_recv.at[i], at_z(lax.rem(z + (1 if i == 0 else nz - 1), nz)))
        for i in range(2)
    ]
    w_x = [
        remote(wg.at[c, x], wg.at[c, x], wx_send.at[i], wx_recv.at[i], at_x(1 if i == 0 else NX - 1))
        for i in range(2)
    ]
    w_relay = []
    for i in range(2):
        ref = wg.at[c, lax.rem(x + (NX - 1 if i == 0 else 1), NX), :, pl.ds(i * (nz // G // 2), nz // G // 2)]
        w_relay.append(
            remote(ref, ref, wx_send.at[2 + i], wx_recv.at[2 + i], at_x(1 if i == 0 else NX - 1))
        )
    w_core = remote(wg.at[c], wg.at[c], wc_send.at[1], wc_recv.at[1], other_core)
    core_copies = [
        remote(pb.at[q, 1 - c], cr.at[q], c_send.at[q], c_recv.at[q], other_core)
        for q in range(n_chunks)
    ]
    x_copies = {
        q: remote(
            xs.at[q // NX, q % NX], xr.at[q // NX, q % NX],
            x_send.at[q // NX, q % NX], x_recv.at[q // NX, q % NX], at_x(1 + q % NX),
        )
        for q in range(n_chunks) if q % NX < NX - 1
    }
    value_copies = [
        remote(
            vs.at[lax.rem(y + i, ny)], vr.at[y], v_send.at[i - 1], v_recv.at[i - 1], at_y(i)
        )
        for i in range(1, ny)
    ]

    def z_copy(h, i):
        return remote(
            zs.at[h, i], zr.at[z], z_send.at[h, i], z_recv.at[z], at_z(i * H + h)
        )

    def row_of(source, field):
        both = meta[source][:, :toks]
        return jnp.where(expert0, both[field:field + 1], both[2 + field:3 + field])

    def spread():
        fetched[4].wait()
        fetched[5].wait()
        for copy in meta_copies:
            copy.wait_recv()
        tables = []
        for s in range(ny):
            slot_col = to_col(row_of(s, 1))
            p_col = to_col(row_of(s, 0))
            place = lax.broadcasted_iota(jnp.int32, (toks, slots * ny), 1)
            mine = (lax.rem(place, ny) == s) & (lax.div(place, ny).astype(F32) == slot_col)
            tables.append(jnp.where(mine, 1.0, 0.0))
            pt[pl.ds(s * toks, toks), :] = jnp.broadcast_to(p_col, (toks, 128))
        table = jnp.concatenate(tables, axis=0).astype(BF16)
        g = jnp.dot(table, saved(gate_ref), preferred_element_type=F32)
        u = jnp.dot(table, saved(up_ref), preferred_element_type=F32)
        gt[...] = g
        ut[...] = u
        hidden = g * jax.nn.sigmoid(g) * u
        wt[...] = (pt[:, :1] * hidden).astype(BF16)

    def saved(ref):
        return ref[...].astype(F32).reshape(slots * ny, hid).astype(BF16)

    def tokens_of(k, h):
        return yb[k, h].astype(F32).reshape(ny * toks, lanes).astype(BF16)

    def multiply(q):
        for way in range(2):
            if hops(q, way):
                ring(q, way, hops(q, way) - 1).wait_recv()
        part = lax.dot_general(
            tokens_of(target_x(q), q // NX), wt[...], (((0,), (0,)), ((), ())),
            preferred_element_type=F32,
        )
        for i in range(nzh):
            for j in range(2):
                lo = (i * 2 + j) * toks
                pb[q, j, i] = part[lo:lo + toks]
        core_copies[q].start()

    def pair(q):
        h, j = q // NX, q % NX
        core_copies[q].wait_recv()
        total = pb[q, c] + cr[q]
        if j < NX - 1:
            xs[h, j] = total.astype(BF16)
            x_copies[q].start()
        else:
            ac[h] = total

    def finish(h):
        total = ac[h]
        for i in range(NX - 1):
            x_copies[h * NX + i].wait_recv()
            total = total + xr[h, i].astype(F32)
        ac[h] = total
        zs[h] = total.astype(BF16)
        for i in range(nzh):
            @pl.when(z != i * H + h)
            def _():
                z_copy(h, i).start()

    def w_first():
        w_pair.wait_recv()
        mine = w_ref[...].astype(F32)
        theirs = wo[...].astype(F32)
        first = jnp.where(c == 0, mine, theirs)
        second = jnp.where(c == 0, theirs, mine)
        both = jnp.concatenate([first, second], axis=0)
        wg[c, x, lax.rem(z, G), lax.div(z, G)] = jnp.where(c == 0, both[:, :half], both[:, half:]).astype(BF16)
        for copy in w_far:
            copy.start()

    def w_near_step():
        for copy in w_far:
            copy.wait_recv()
        for copy in w_near:
            copy.start()

    def w_second():
        for copy in w_near:
            copy.wait_recv()
        for copy in w_x:
            copy.start()

    def w_third():
        for copy, relay in zip(w_x, w_relay):
            copy.wait_recv()
            relay.start()

    def w_fourth():
        for relay in w_relay:
            relay.wait_recv()
        w_core.start()

    def activations():
        w_core.wait_recv()
        dh = jnp.zeros((ny * toks, hid), F32)
        for k in range(NX):
            for h in range(H):
                weights = jnp.concatenate(
                    [
                        jnp.concatenate(
                            [wg[i, k, zz % G, zz // G] for zz in range(h, nz, H)], axis=0
                        )
                        for i in range(2)
                    ],
                    axis=1,
                )
                dh = dh + jnp.dot(
                    tokens_of(k, h)[:, :chan], weights, preferred_element_type=F32
                )
        g, u, p = gt[...], ut[...], pt[:, :1]
        sig = jax.nn.sigmoid(g)
        act = g * sig
        hidden = act * u
        scaled = p * dh
        up_tok = (scaled * act).astype(BF16)
        gate_tok = (scaled * u * sig * (1.0 + g * (1.0 - sig))).astype(BF16)
        value = jnp.sum(hidden * dh, axis=1, keepdims=True)
        for s in range(ny):
            row = to_row(value[s * toks:(s + 1) * toks])
            vs[s, :, :toks] = jnp.broadcast_to(row, (8, toks))
        for copy in value_copies:
            copy.start()
        vr[y] = vs[y]
        packs = []
        for s in range(ny):
            place = lax.broadcasted_iota(jnp.int32, (slots * ny, toks), 0)
            mine = (lax.rem(place, ny) == s) & (lax.div(place, ny).astype(F32) == row_of(s, 1))
            packs.append(jnp.where(mine, 1.0, 0.0))
        pack = jnp.concatenate(packs, axis=1).astype(BF16)
        for ref, values in ((ug_ref, up_tok), (gg_ref, gate_tok)):
            packed = jnp.dot(pack, values, preferred_element_type=F32)
            ref[...] = packed.reshape(slots, ny, hid).astype(BF16)

    fetched[3].wait()
    w_pair.start()
    depth = ny // 2
    work = {SPREAD: [spread]}
    for slot, step in zip(W_SLOTS, (w_first, w_near_step, w_second, w_third, w_fourth)):
        work.setdefault(slot, []).append(step)
    last = n_chunks - 1 + SKEW * (depth - 1) + LAG
    for t in range(last + 1):
        for q in range(n_chunks):
            if max(0, q - AHEAD) == t:
                for way in range(2):
                    if hops(q, way):
                        ring(q, way, 0).start()
        if t == 0:
            for copy in meta_copies:
                copy.start()
        for s in range(1, depth):
            q = t - SKEW * (s - 1)
            if 0 <= q < n_chunks:
                for way in range(2):
                    if s < hops(q, way):
                        ring(q, way, s - 1).wait_recv()
                        ring(q, way, s).start()
        for step in work.get(t, []):
            step()
        q = t - SKEW * (depth - 1)
        if 0 <= q < n_chunks:
            multiply(q)
        q = t - SKEW * (depth - 1) - LAG
        if 0 <= q < n_chunks:
            if q == n_chunks - 1:
                activations()
            pair(q)
        q = t - SKEW * (depth - 1) - LAG - WAIT_X
        if q >= 0 and q % NX == NX - 1:
            finish(q // NX)
    for q in range(last + 1 - SKEW * (depth - 1) - LAG - WAIT_X, n_chunks):
        if q % NX == NX - 1:
            finish(q // NX)

    for copy in value_copies:
        copy.wait_recv()
    held = jnp.zeros(route.shape, F32)
    share = ny // FLIGHT
    for e in range(FLIGHT):
        row = vr[e * share][0:1, :toks]
        for i in range(1, share):
            row = row + vr[e * share + i][0:1, :toks]
        held = held + jnp.where(route == e, row, 0.0)
    pg_ref[...] = held

    total = ac[zh, zi]
    for i in range(1, nz):
        source = lax.rem(z + i, nz)
        remote(zs.at[0, 0], zr.at[source], z_send.at[0, 0], z_recv.at[source], other_core).wait_recv()
        total = total + zr[source].astype(F32)
    dg_ref[...] = total

    for q in range(n_chunks):
        for way in range(2):
            for s in range(hops(q, way)):
                ring(q, way, s).wait_send()
    for copy in (
        meta_copies + [w_pair] + w_far + w_near + w_x + w_relay + [w_core] + core_copies
        + list(x_copies.values()) + value_copies
    ):
        copy.wait_send()
    for h in range(H):
        for i in range(nzh):
            @pl.when(z != i * H + h)
            def _():
                z_copy(h, i).wait_send()


def hand_over(a, b, c, d, a_out, b_out, c_out, d_out):
    for src, dst in ((a, a_out), (b, b_out), (c, c_out), (d, d_out)):
        dst[...] = src[...]


def body(grad_out, routing, probs, down_weight, gate_saved, up_saved):
    ny, n_dp = lax.axis_size("expert"), lax.axis_size("dp")
    nz = n_dp // (2 * NX)
    toks, width = grad_out.shape
    slots, hid = gate_saved.shape[1:]
    saved = (slots, ny, hid)
    top = routing.shape[1]
    half = hid // 2
    nzh = nz // H
    chan = nzh * 2 * toks
    lanes = -(-chan // 128) * 128
    n_chunks = NX * H
    depth = ny // 2
    dma = pltpu.SemaphoreType.DMA
    vmem = pl.BlockSpec(memory_space=pltpu.VMEM)
    scratch = [
        pltpu.VMEM(grad_out.shape, BF16),
        pltpu.VMEM((top, toks), jnp.int32),
        pltpu.VMEM((top, toks), BF16),
        pltpu.VMEM(down_weight.shape, BF16),
        pltpu.VMEM(saved, BF16),
        pltpu.VMEM(saved, BF16),
        dma((6,)),
        pltpu.VMEM((NX, H, ny, toks, lanes), BF16),
        pltpu.VMEM((ny, 8, 128), F32),
        pltpu.VMEM((ny * toks, hid), BF16),
        pltpu.VMEM((ny * toks, hid), F32),
        pltpu.VMEM((ny * toks, hid), F32),
        pltpu.VMEM((ny * toks, 128), F32),
        pltpu.VMEM((toks, hid), BF16),
        pltpu.VMEM((2, NX, G, nz // G, 2 * toks, half), BF16),
        pltpu.VMEM((n_chunks, 2, nzh, toks, hid), F32),
        pltpu.VMEM((n_chunks, nzh, toks, hid), F32),
        pltpu.VMEM((H, NX - 1, nzh, toks, hid), BF16),
        pltpu.VMEM((H, NX - 1, nzh, toks, hid), BF16),
        pltpu.VMEM((H, nzh, toks, hid), BF16),
        pltpu.VMEM((nz, toks, hid), BF16),
        pltpu.VMEM((H, nzh, toks, hid), F32),
        pltpu.VMEM((ny, 8, 128), F32),
        pltpu.VMEM((ny, 8, 128), F32),
        dma((n_chunks, 2, depth)), dma((n_chunks, 2, depth)),
        dma((ny - 1,)), dma((ny - 1,)),
        dma((2,)), dma((2,)),
        dma((nz // G - 1,)), dma((nz // G - 1,)),
        dma((2,)), dma((2,)),
        dma((4,)), dma((4,)),
        dma((n_chunks,)), dma((n_chunks,)),
        dma((H, NX - 1)), dma((H, NX - 1)),
        dma((H, nzh)), dma((nz,)),
        dma((ny - 1,)), dma((ny - 1,)),
    ]
    shapes = (
        jax.ShapeDtypeStruct(down_weight.shape, F32),
        jax.ShapeDtypeStruct(saved, BF16),
        jax.ShapeDtypeStruct(saved, BF16),
        jax.ShapeDtypeStruct((top, toks), F32),
    )
    parts = pl.pallas_call(
        functools.partial(kernel, (ny, nz)),
        out_shape=shapes,
        in_specs=[pl.BlockSpec(memory_space=pl.ANY)] * 6,
        out_specs=(vmem,) * 4,
        scratch_shapes=scratch,
        compiler_params=pltpu.CompilerParams(
            collective_id=0, has_side_effects=True, vmem_limit_bytes=63 * 1024 * 1024
        ),
    )(
        grad_out, routing.T, probs.T, down_weight,
        jnp.transpose(gate_saved, (1, 0, 2)), jnp.transpose(up_saved, (1, 0, 2)),
    )
    down_grad, gate_grad, up_grad, prob_grad = pl.pallas_call(
        hand_over,
        out_shape=shapes,
        in_specs=[vmem] * 4,
        out_specs=(vmem,) * 4,
        compiler_params=pltpu.CompilerParams(vmem_limit_bytes=63 * 1024 * 1024),
    )(*parts)
    return (
        down_grad, jnp.transpose(gate_grad, (1, 0, 2)), jnp.transpose(up_grad, (1, 0, 2)),
        prob_grad.T,
    )


def solution(mesh):
    in_specs = (
        P(("dp", "expert"), None),
        P(("dp", "expert"), None),
        P(("dp", "expert"), None),
        P("dp", "expert"),
        P("dp", None, "expert"),
        P("dp", None, "expert"),
    )
    out_specs = (
        P("dp", "expert"),
        P("dp", None, "expert"),
        P("dp", None, "expert"),
        P(("dp", "expert"), None),
    )
    return jax.shard_map(body, mesh=mesh, in_specs=in_specs, out_specs=out_specs, check_vma=False)
```
